128 devices in a mesh: dp: 32 (over x, y, z_lo), tensor: 4 (over z_hi, core).
Axes of the slice: x: 4, y: 4, z: 4 (z_hi: 2, z_lo: 2; z = z_hi * 2 + z_lo), core: 2. Of those that a mesh axis runs over, the one named last changes fastest.
Arguments:
- activations: bfloat16 [1024, 128, 2048], P('dp', None, 'tensor'), may hold values from -6 to 6
- out_grads: bfloat16 [1024, 128, 8192], P('dp', None, 'tensor'), may hold values from -6 to 6
- lengths: int32 [1024], P('dp'), may hold values from 1 to 128
- proj_in: bfloat16 [2048, 64], P('tensor'), may hold values from -0.125 to 0.125
- proj_out: bfloat16 [8192, 64], P('tensor'), may hold values from -0.0625 to 0.0625
- query_grads: bfloat16 [2048, 4096], P('dp', 'tensor'), may hold values from -400 to 400, as said below
Outputs:
- scores: float32 [1024, 2048], P('dp')
The draws below stay inside these ranges and needn't reach their ends.
Inputs may be any that keep to these rules, and one draw needn't show every extreme that they name: `query_grads`: entries have different typical sizes from column to column and from row to row.
All inputs are finite; a program needn't handle non-finite values.
Results may differ from the reference program's by a relative error of at most 0.005.
Values may be sent and summed in bfloat16 or wider, within the bound.
A program may use at most 64 MiB of HBM per device.

```python
import jax
import jax.numpy as jnp
from jax import lax

D = 2048
FF = 8192
RANK = 64
LEN = 128
TRAIN = 1024
QUERY = 2048


def draw_query_grads(key, part):
    key = jax.random.fold_in(key, 11)
    key_base, key_column, key_row = jax.random.split(key, 3)
    column_scale = jnp.exp(jax.random.uniform(key_column, (1, RANK * RANK), jnp.float32, 0.0, 2.3))
    base_value = jnp.clip(jax.random.normal(key_base, (QUERY, RANK * RANK), jnp.float32), -4.0, 4.0)
    row_scale = jnp.exp(jax.random.uniform(key_row, (QUERY, 1), jnp.float32, 0.0, 2.3))
    return (base_value * column_scale * row_scale).astype(jnp.bfloat16)


def plant(drawn, stream_key, smallest, largest):
    place = [jax.random.randint(jax.random.fold_in(stream_key, axis), (), 0, length) for axis, length in enumerate(drawn.shape)]
    main_axis = drawn.shape.index(max(drawn.shape))
    beside = place[:main_axis] + [(place[main_axis] + 1) % drawn.shape[main_axis]] + place[main_axis + 1:]
    return drawn.at[tuple(place)].set(smallest).at[tuple(beside)].set(largest)


def steps_of(stream_key, dims, shards, low, high):
    def one(dim, blocks):
        draws = jax.random.uniform(jax.random.fold_in(jax.random.fold_in(stream_key, 6), dim), (blocks,), jnp.float32, low / len(shards), high / len(shards))
        return jnp.repeat(jnp.exp(draws), dims[dim] // blocks).reshape((-1,) + (1,) * (len(dims) - dim - 1))

    level = one(*shards[0])
    for cut in shards[1:]:
        level = level * one(*cut)
    return level


def noise(own_key, shape, scale, bound, cuts=(), held_as=jnp.bfloat16):
    values = jax.random.normal(own_key, shape, jnp.float32) * scale
    if len(cuts) > 0:
        values = steps_of(own_key, shape, cuts, -0.22, 0.18) * values
    return jnp.clip(values, min=-bound, max=bound).astype(held_as)


def setup_inputs(seed: int = 0) -> dict:
    key_list = jax.random.split(jax.random.key(seed), 7)
    activations = noise(key_list[0], (TRAIN, LEN, D), 1.0, 6.0, ((0, 32), (2, 4)))
    out_grads = noise(key_list[1], (TRAIN, LEN, FF), 1.0, 6.0, ((0, 32), (2, 4)))
    lengths = plant(jax.random.randint(key_list[2], (TRAIN,), 1, LEN + 1), jax.random.fold_in(key_list[2], 1), 1, LEN).astype(jnp.int32)
    proj_in = noise(key_list[3], (D, RANK), D ** -0.5, 0.125, ((0, 4),))
    proj_out = noise(key_list[4], (FF, RANK), FF ** -0.5, 0.0625, ((0, 4),))
    query_grads = draw_query_grads(jax.random.fold_in(key_list[6], 71), 0)
    return {"activations": activations, "out_grads": out_grads, "lengths": lengths, "proj_in": proj_in, "proj_out": proj_out, "query_grads": query_grads}


eps = 1e-06

def reference(activations, out_grads, lengths, proj_in, proj_out, query_grads):
    valid_mask = (lax.broadcasted_iota(jnp.int32, (TRAIN, LEN), 1) < lengths[:, None]).astype(jnp.float32)
    out_side = jnp.dot(out_grads.reshape(TRAIN * LEN, FF), proj_out, preferred_element_type=jnp.float32)
    out_side = (out_side.reshape(TRAIN, LEN, RANK) * valid_mask[:, :, None]).astype(jnp.bfloat16)
    in_side = jnp.dot(activations.reshape(TRAIN * LEN, D), proj_in, preferred_element_type=jnp.float32)
    in_side = in_side.reshape(TRAIN, LEN, RANK).astype(jnp.bfloat16)
    train_grads = jnp.einsum('tlr,tls->trs', out_side.astype(jnp.float32), in_side.astype(jnp.float32))
    train_grads = train_grads.astype(jnp.bfloat16).reshape(TRAIN, RANK * RANK)
    train_sq = lax.optimization_barrier(jnp.sum(jnp.square(train_grads.astype(jnp.float32)), axis=1))
    query_sq = lax.optimization_barrier(jnp.sum(jnp.square(query_grads.astype(jnp.float32)), axis=1))
    products = lax.dot_general(train_grads, query_grads, (((1,), (1,)), ((), ())), preferred_element_type=jnp.float32)
    return RANK * products * lax.rsqrt(train_sq + eps)[:, None] * lax.rsqrt(query_sq + eps)[None, :]
```

```python
import jax
import jax.numpy as jnp
from jax import lax
from jax.experimental import pallas as pl
from jax.experimental.pallas import tpu as pltpu
from jax.sharding import PartitionSpec as P

eps = 1e-06
f32 = jnp.float32
bf16 = jnp.bfloat16
MESH = pl.DeviceIdType.MESH

SIDE = 4
CHUNKS = 8
AHEAD = 3
ENTER = 1
REDUCE_LAG = 2
QUERY_STEPS = (2,5,6,7)
LAG = 7
RING = ((2, 0), (2, 1), (1, 0), (1, 1), (3, 0), (3, 1), (0, 1))
AROUND = (1, 3, 2)


def dot(left, right):
    return jnp.dot(left, right, preferred_element_type=f32)


def kernel(
    lengths_in, out_grads, activations, proj_in_in, proj_out_in, queries_in,
    scores,
    lengths, query_grads, proj_in_t, proj_out_t, out_held, act_held, w_out, w_in,
    own_part, pair_send, pair_recv, reduce_send, reduce_recv,
    grads_send, grads_recv, grads_wide, train,
    queries, square_part, square_send, square_recv,
    part_send, part_recv, part_rows, spread,
    small_sem, load_sem, pair_ssem, pair_rsem, reduce_ssem, reduce_rsem,
    grads_ssem, grads_rsem, swap_sem,
    qa_ssem, qa_rsem, qb_ssem, qb_rsem,
    square_ssem, square_rsem, part_ssem, part_rsem,
):
    dp = lax.axis_index("dp")
    tensor = lax.axis_index("tensor")
    x, y, z_lo = dp // 8, (dp // 2) % 4, dp % 2
    z_hi, core = tensor // 2, tensor % 2
    z = z_hi * 2 + z_lo
    here = x * SIDE + y

    def device(x, y, z, core):
        return (x * 8 + y * 2 + z % 2, (z // 2) * 2 + core)

    def ring_peer(step_z, step_core):
        return (z + step_z) % SIDE, (core + step_core) % 2

    def grads_place(z, core):
        return 1 - z % 2, core * 2 + z // 2

    def part_place(z, core):
        return (z // 2) * 4 + (z % 2) * 2 + core

    sibling = device(x, y, z, 1 - core)
    ring = [ring_peer(*steps) for steps in RING]
    ring_ids = [device(x, y, *peer) for peer in ring]
    x_ids = [device((x + step) % SIDE, y, z, core) for step in AROUND]
    y_ids = [device(x, (y + step) % SIDE, z, core) for step in AROUND]

    def remote(src, dst, send_sem, recv_sem, to):
        return pltpu.make_async_remote_copy(
            src_ref=src, dst_ref=dst, send_sem=send_sem, recv_sem=recv_sem,
            device_id=to, device_id_type=MESH,
        )

    def loads(chunk):
        for half in range(2):
            rows = pl.ds(pl.multiple_of((core + half) % 2 * 256, 256), 256)
            held = pl.ds(half * 256, 256)
            yield pltpu.make_async_copy(
                out_grads.at[chunk, rows], out_held.at[chunk, held], load_sem.at[chunk * 4 + half]
            )
            yield pltpu.make_async_copy(
                activations.at[chunk, rows], act_held.at[chunk, held], load_sem.at[chunk * 4 + 2 + half]
            )

    small = [
        pltpu.make_async_copy(proj_out_in, proj_out_t, small_sem.at[0]),
        pltpu.make_async_copy(proj_in_in, proj_in_t, small_sem.at[1]),
        pltpu.make_async_copy(lengths_in, lengths, small_sem.at[2]),
        pltpu.make_async_copy(queries_in, query_grads, small_sem.at[3]),
    ]
    for load in small:
        load.start()
    for load in small:
        load.wait()
    for chunk in range(AHEAD):
        for load in loads(chunk):
            load.start()

    barrier = pltpu.get_barrier_semaphore()
    peers = ring_ids + x_ids + y_ids
    for peer in peers:
        pl.semaphore_signal(barrier, inc=1, device_id=peer, device_id_type=MESH)

    rank_row = lax.broadcasted_iota(jnp.int32, (64, 128), 0)
    lane = lax.broadcasted_iota(jnp.int32, (64, 128), 1)
    place_out = (lane == (rank_row % 2) * 32 + rank_row // 2).astype(bf16)
    place_in = (lane == rank_row + 64).astype(bf16)
    columns = (((0,), (0,)), ((), ()))
    w_in[...] = lax.dot_general(proj_in_t[...], place_in, columns, preferred_element_type=f32).astype(bf16)
    w_out[...] = lax.dot_general(proj_out_t[...], place_out, columns, preferred_element_type=f32).astype(bf16)

    half_columns = pl.ds(pl.multiple_of(core * 1024, 1024), 1024)
    swap_out = remote(
        query_grads.at[pl.ds(pl.multiple_of((1 - core) * 32, 32), 32)],
        queries.at[here, :, half_columns],
        swap_sem.at[0], swap_sem.at[1], sibling,
    )
    swap_own = pltpu.make_async_copy(
        query_grads.at[pl.ds(pl.multiple_of(core * 32, 32), 32)],
        queries.at[here, :, half_columns],
        swap_sem.at[2],
    )

    def query_half(half, owner, ssem, rsem, index, to):
        rows = queries.at[owner, pl.ds(half * 16, 16)]
        return remote(rows, rows, ssem.at[index], rsem.at[owner], to)

    def a_send(index, owner, to):
        return query_half(0, owner, qa_ssem, qa_rsem, index, to)

    def b_send(index, owner, to):
        return query_half(1, owner, qb_ssem, qb_rsem, index, to)

    def enter():
        pl.semaphore_wait(barrier, len(peers))
        swap_out.start()
        swap_own.start()
        for chunk in range(ENTER + 1):
            pair_copy(chunk).start()

    def queries_first():
        swap_own.wait()
        swap_out.wait()
        for i in range(3):
            a_send(i, here, x_ids[i]).start()
            b_send(i, here, y_ids[i]).start()
        for i in range(3):
            a_send(3 + i, here, y_ids[i]).start()
            b_send(3 + i, here, x_ids[i]).start()

    def queries_second(k):
        step = AROUND[k]
        a_owner = ((x + step) % SIDE) * SIDE + y
        a_send(0, a_owner, sibling).wait_recv()
        for i in range(3):
            a_send(6 + k * 3 + i, a_owner, y_ids[i]).start()
        b_owner = x * SIDE + (y + step) % SIDE
        b_send(0, b_owner, sibling).wait_recv()
        for i in range(3):
            b_send(6 + k * 3 + i, b_owner, x_ids[i]).start()

    def queries_last():
        for step in AROUND:
            for other in (0,) + AROUND:
                a_owner = ((x + other) % SIDE) * SIDE + (y + step) % SIDE
                a_send(0, a_owner, sibling).wait_recv()
                b_owner = ((x + step) % SIDE) * SIDE + (y + other) % SIDE
                b_send(0, b_owner, sibling).wait_recv()

    token = lax.broadcasted_iota(jnp.int32, (128, 128), 0)

    def pair_copy(chunk):
        return remote(pair_send.at[chunk], pair_recv.at[chunk], pair_ssem.at[chunk], pair_rsem.at[chunk], sibling)

    def reduce_copy(chunk, owner_hi, source_hi):
        to = device(x, y, owner_hi * 2 + 1 - z_lo, core)
        return remote(
            reduce_send.at[chunk, owner_hi], reduce_recv.at[chunk, source_hi],
            reduce_ssem.at[chunk * 2 + owner_hi], reduce_rsem.at[chunk * 2 + source_hi], to,
        )

    def project(chunk):
        for load in loads(chunk):
            load.wait()

        @pl.when(chunk + AHEAD < CHUNKS)
        def _():
            for load in loads(chunk + AHEAD):
                load.start()

        total = dot(out_held[chunk], w_out[...])
        total += dot(act_held[chunk], w_in[...])
        kept = []
        for place in range(4):
            owner = ((core + place // 2) % 2) * 2 + place % 2
            length = lengths[chunk * 4 + owner]
            kept.append(jnp.where(token < length, total[place * 128 : place * 128 + 128], 0.0))
        own_part[chunk, 0:128] = kept[0]
        own_part[chunk, 128:256] = kept[1]
        pair_send[chunk, 0:128] = kept[2]
        pair_send[chunk, 128:256] = kept[3]
    def reduce(chunk):
        pair_copy(chunk).wait_recv()
        for owner_hi in range(2):
            rows = slice(owner_hi * 128, owner_hi * 128 + 128)
            total = own_part[chunk, rows] + pair_recv[chunk, rows]
            largest = jnp.max(jnp.abs(total), axis=0, keepdims=True)
            power = jnp.floor(jnp.log2(jnp.maximum(largest, 1e-30))) + 1.0
            scaled = jnp.round(total * jnp.exp2(15.0 - power))
            coded = jnp.clip(scaled, -32767.0, 32767.0).astype(jnp.int32).astype(jnp.int16)
            reduce_send[chunk, owner_hi, 0:128] = coded
            reduce_send[chunk, owner_hi, 128:144] = jnp.broadcast_to(power, (16, 128)).astype(jnp.int32).astype(jnp.int16)
            reduce_copy(chunk, owner_hi, z_hi).start()

    def outer(chunk):
        for source_hi in range(2):
            reduce_copy(chunk, 0, source_hi).wait_recv()
        total = jnp.zeros((128, 128), f32)
        for source_hi in range(2):
            power = reduce_recv[chunk, source_hi, 128:144].astype(jnp.int32)[0:1].astype(f32)
            total += reduce_recv[chunk, source_hi, 0:128].astype(jnp.int32).astype(f32) * jnp.exp2(power - 15.0)
        sides = total.astype(bf16)
        wide = sides.astype(f32)
        lanes = lax.broadcasted_iota(jnp.int32, (128, 128), 1)
        in_twice = jnp.where(lanes < 64, pltpu.roll(wide, 64, 1), wide).astype(bf16)
        both = lax.dot_general(sides, in_twice, columns, preferred_element_type=f32)
        grads = jnp.where(lanes[0:32] < 64, both[0:32], both[32:64])
        squares = jnp.square(grads.astype(bf16).astype(f32))
        square = jnp.sum(jnp.sum(squares, axis=0, keepdims=True), axis=1, keepdims=True)
        scaled = (grads * (64.0 * lax.rsqrt(square + eps))).astype(bf16)
        grads_send[0, chunk] = scaled[0:16]
        grads_send[1, chunk] = scaled[16:32]

    def grads_copy(batch, index, peer, source, to):
        block, owner = source
        rows = pl.ds(batch * 4, 4)
        return remote(
            grads_send.at[peer[0] // 2, rows], grads_recv.at[block, rows, owner],
            grads_ssem.at[batch * 7 + index], grads_rsem.at[batch * 8 + block * 4 + owner], to,
        )

    def grads_out(batch):
        for i in range(7):
            grads_copy(batch, i, ring[i], grads_place(z, core), ring_ids[i]).start()

    def step(s, carry):
        pl.when(s < CHUNKS)(lambda: project(s))
        pl.when(s == ENTER)(enter)
        pl.when((s > ENTER) & (s < CHUNKS))(lambda: pair_copy(s).start())
        pl.when(s == QUERY_STEPS[0])(queries_first)
        pl.when((s >= REDUCE_LAG) & (s < CHUNKS + REDUCE_LAG))(lambda: reduce(s - REDUCE_LAG))
        for k in range(3):
            pl.when(s == QUERY_STEPS[1 + k])(lambda: queries_second(k))
        pl.when(s >= LAG)(lambda: outer(s - LAG))
        pl.when(s == LAG + 3)(lambda: grads_out(0))
        pl.when(s == LAG + 7)(lambda: grads_out(1))
        return carry

    lax.fori_loop(0, CHUNKS + LAG, step, 0)

    spread[...] = jnp.zeros_like(spread)
    query_row = lax.broadcasted_iota(jnp.int32, (32, 128), 0)
    query_lane = lax.broadcasted_iota(jnp.int32, (32, 128), 1)
    for source in range(8):
        at = ((source // 2) % 2) * 64 + (source % 2) * 32
        pattern = (query_lane == query_row + at).astype(bf16)
        for column in range(4):
            spread[source * 128 + column * 32 : source * 128 + column * 32 + 32, column * 128 : column * 128 + 128] = pattern

    queries_last()

    def square_rows(block, carry):
        wide = queries[block].astype(f32)
        squares = wide * wide
        total = squares[:, 0:128]
        for column in range(1, 16):
            total += squares[:, column * 128 : column * 128 + 128]
        square_part[pl.ds(pl.multiple_of(block * 32, 32), 32)] = total
        return carry

    lax.fori_loop(0, 16, square_rows, 0)
    row = lax.broadcasted_iota(jnp.int32, (8, 128), 0)
    squares = jnp.zeros((8, 128), f32)
    for group in range(4):
        sums = lax.dot_general(
            jnp.ones((8, 128), f32), square_part[group * 128 : group * 128 + 128], (((1,), (1,)), ((), ())),
            precision=lax.Precision.HIGHEST, preferred_element_type=f32,
        )
        squares = jnp.where(row == group, sums, squares)
    square_send[...] = squares

    def square_copy(index, place, to):
        return remote(square_send, square_recv.at[place], square_ssem.at[index], square_rsem.at[place], to)

    own_place = part_place(z, core)
    for i in range(7):
        square_copy(i, own_place, ring_ids[i]).start()
    square_recv[own_place] = squares

    own_grads = grads_place(z, core)
    for n in range(CHUNKS):
        grads_recv[own_grads[0], n, own_grads[1]] = grads_send[z_hi, n]
    for batch in range(2):
        for i in range(7):
            grads_copy(batch, i, ring[i], grads_place(*ring[i]), ring_ids[i]).wait_recv()
    grads_wide[...] = grads_recv[...].reshape(1024, 128).astype(f32)
    for j in range(16):
        train[:, j * 128 : j * 128 + 128] = grads_wide[pl.ds(j, 64, stride=16), :].astype(bf16)

    products = lax.dot_general(
        train[...], queries[...].reshape(512, 2048), (((1,), (1,)), ((), ())), preferred_element_type=f32
    )
    part_send[...] = products.astype(bf16).reshape(2, 32, 512)

    def part_copy(index, peer, place, to):
        return remote(
            part_send.at[peer[0] % 2], part_recv.at[place], part_ssem.at[index], part_rsem.at[place], to
        )

    for i in range(7):
        part_copy(i, ring[i], own_place, ring_ids[i]).start()
    part_recv[own_place] = part_send[z_lo]

    for chunk in range(CHUNKS):
        pair_copy(chunk).wait_send()
        for owner_hi in range(2):
            reduce_copy(chunk, owner_hi, 0).wait_send()
    for batch in range(2):
        for i in range(7):
            grads_copy(batch, i, ring[i], own_grads, ring_ids[i]).wait_send()
    for i in range(15):
        a_send(i, here, sibling).wait_send()
        b_send(i, here, sibling).wait_send()
    for i in range(7):
        square_copy(i, own_place, ring_ids[i]).wait_send()

    for i in range(7):
        square_copy(i, part_place(*ring[i]), ring_ids[i]).wait_recv()
    left = jnp.concatenate([square_recv[place] for place in range(8)], axis=1)
    pieces = []
    for _ in range(3):
        piece = left.astype(bf16)
        pieces.append(piece)
        left = left - piece.astype(f32)
    spread_squares = sum(dot(piece, spread[...]) for piece in pieces)
    scales = lax.rsqrt(spread_squares + eps)

    for i in range(7):
        part_copy(i, ring[i], part_place(*ring[i]), ring_ids[i]).wait_recv()
    for place in range(8):
        for group in range(4):
            part_rows[group * 32 : group * 32 + 32, place * 128 : place * 128 + 128] = part_recv[
                place, :, group * 128 : group * 128 + 128
            ]
    result = dot(part_rows[...], spread[...])
    for group in range(4):
        scores[:, group * 512 : group * 512 + 512] = result[group * 32 : group * 32 + 32] * scales[group : group + 1]
    for i in range(7):
        part_copy(i, ring[i], own_place, ring_ids[i]).wait_send()


def on_device(activations, out_grads, lengths, proj_in, proj_out, query_grads):
    dma = pltpu.SemaphoreType.DMA
    vmem = pl.BlockSpec(memory_space=pltpu.VMEM)
    hbm = pl.BlockSpec(memory_space=pltpu.HBM)
    return pl.pallas_call(
        kernel,
        out_shape=jax.ShapeDtypeStruct((32, 2048), f32),
        in_specs=[hbm] * 6,
        out_specs=vmem,
        scratch_shapes=[
            pltpu.SMEM((32,), jnp.int32),
            pltpu.VMEM((64, 1024), bf16),
            pltpu.VMEM((64, 512), bf16),
            pltpu.VMEM((64, 2048), bf16),
            pltpu.VMEM((8, 512, 2048), bf16),
            pltpu.VMEM((8, 512, 512), bf16),
            pltpu.VMEM((2048, 128), bf16),
            pltpu.VMEM((512, 128), bf16),
            pltpu.VMEM((8, 256, 128), f32),
            pltpu.VMEM((8, 256, 128), f32),
            pltpu.VMEM((8, 256, 128), f32),
            pltpu.VMEM((8, 2, 144, 128), jnp.int16),
            pltpu.VMEM((8, 2, 144, 128), jnp.int16),
            pltpu.VMEM((2, 8, 16, 128), bf16),
            pltpu.VMEM((2, 8, 4, 16, 128), bf16),
            pltpu.VMEM((1024, 128), f32),
            pltpu.VMEM((64, 2048), bf16),
            pltpu.VMEM((16, 32, 2048), bf16),
            pltpu.VMEM((512, 128), f32),
            pltpu.VMEM((8, 128), f32),
            pltpu.VMEM((8, 8, 128), f32),
            pltpu.VMEM((2, 32, 512), bf16),
            pltpu.VMEM((8, 32, 512), bf16),
            pltpu.VMEM((128, 1024), bf16),
            pltpu.VMEM((1024, 512), bf16),
            dma((4,)),
            dma((32,)),
            dma((8,)),
            dma((8,)),
            dma((16,)),
            dma((16,)),
            dma((14,)),
            dma((16,)),
            dma((3,)),
            dma((15,)),
            dma((16,)),
            dma((15,)),
            dma((16,)),
            dma((7,)),
            dma((8,)),
            dma((7,)),
            dma((8,)),
        ],
        compiler_params=pltpu.CompilerParams(
            collective_id=0, has_side_effects=True, vmem_limit_bytes=64 * 2**20 - 512 * 1024
        ),
    )(
        lengths,
        out_grads.reshape(8, 512, 2048),
        activations.reshape(8, 512, 512),
        proj_in.T,
        proj_out.T,
        query_grads,
    )


def solution(mesh):
    placed = (
        P("dp", None, "tensor"),
        P("dp", None, "tensor"),
        P("dp"),
        P("tensor", None),
        P("tensor", None),
        P("dp", "tensor"),
    )
    return jax.shard_map(
        on_device, mesh=mesh, in_specs=placed, out_specs=P("dp", None), check_vma=False
    )
```

```python
import functools

import jax
import jax.numpy as jnp
from jax import lax
from jax.experimental import pallas as pl
from jax.experimental.pallas import tpu as pltpu
from jax.sharding import PartitionSpec as P

eps = 1e-06
f32 = jnp.float32
bf16 = jnp.bfloat16
MESH = pl.DeviceIdType.MESH

SIDE = 4
CHUNKS = 8
AHEAD = 3
REDUCE_LAG = 2
QUERY_STEPS = (1, 5, 8, 10, 12)
BATCHES = ((0, 4), (4, 7), (7, 8))
LAG = 7
RING = ((2, 0), (2, 1), (1, 0), (1, 1), (3, 0), (3, 1), (0, 1))


def dot(left, right):
    return jnp.dot(left, right, preferred_element_type=f32)


def kernel(
    lengths_in, out_grads, activations, proj_in_in, proj_out_in, queries_in,
    scores,
    lengths, query_grads, proj_in_t, proj_out_t, out_held, act_held, w_out, w_in,
    own_part, pair_send, pair_recv, reduce_send, reduce_recv,
    grads_send, grads_recv, grads_wide, train,
    queries, square_part, square_send, square_recv,
    part_send, part_recv, part_rows, spread,
    small_sem, load_sem, pair_ssem, pair_rsem, reduce_ssem, reduce_rsem,
    grads_ssem, grads_rsem, swap_sem,
    query_ssem, query_rsem,
    square_ssem, square_rsem, part_ssem, part_rsem,
):
    dp = lax.axis_index("dp")
    tensor = lax.axis_index("tensor")
    x, y, z_lo = dp // 8, (dp // 2) % 4, dp % 2
    z_hi, core = tensor // 2, tensor % 2
    z = z_hi * 2 + z_lo
    here = x * SIDE + y

    def device(x, y, z, core):
        return (x * 8 + y * 2 + z % 2, (z // 2) * 2 + core)

    def ring_peer(step_z, step_core):
        return (z + step_z) % SIDE, (core + step_core) % 2

    def grads_place(z, core):
        return 1 - z % 2, core * 2 + z // 2

    def part_place(z, core):
        return (z // 2) * 4 + (z % 2) * 2 + core

    sibling = device(x, y, z, 1 - core)
    ring = [ring_peer(*steps) for steps in RING]
    ring_ids = [device(x, y, *peer) for peer in ring]
    around_ids = [device((x + step) % SIDE, y, z, core) for step in (1, 2, 3)]
    around_ids += [device(x, (y + step) % SIDE, z, core) for step in (1, 2, 3)]

    def remote(src, dst, send_sem, recv_sem, to):
        return pltpu.make_async_remote_copy(
            src_ref=src, dst_ref=dst, send_sem=send_sem, recv_sem=recv_sem,
            device_id=to, device_id_type=MESH,
        )

    barrier = pltpu.get_barrier_semaphore()
    peers = ring_ids + around_ids
    for peer in peers:
        pl.semaphore_signal(barrier, inc=1, device_id=peer, device_id_type=MESH)

    def loads(chunk):
        for half in range(2):
            rows = pl.ds(pl.multiple_of((core + half) % 2 * 256, 256), 256)
            held = pl.ds(half * 256, 256)
            yield pltpu.make_async_copy(
                out_grads.at[chunk, rows], out_held.at[chunk, held], load_sem.at[chunk * 4 + half]
            )
            yield pltpu.make_async_copy(
                activations.at[chunk, rows], act_held.at[chunk, held], load_sem.at[chunk * 4 + 2 + half]
            )

    small = [
        pltpu.make_async_copy(proj_out_in, proj_out_t, small_sem.at[0]),
        pltpu.make_async_copy(proj_in_in, proj_in_t, small_sem.at[1]),
        pltpu.make_async_copy(lengths_in, lengths, small_sem.at[2]),
        pltpu.make_async_copy(queries_in, query_grads, small_sem.at[3]),
    ]
    for load in small + list(loads(0)):
        load.start()
    for load in small:
        load.wait()
    for chunk in range(1, AHEAD):
        for load in loads(chunk):
            load.start()

    rank_row = lax.broadcasted_iota(jnp.int32, (64, 128), 0)
    lane = lax.broadcasted_iota(jnp.int32, (64, 128), 1)
    place_out = (lane == (rank_row % 2) * 32 + rank_row // 2).astype(bf16)
    place_in = (lane == rank_row + 64).astype(bf16)
    columns = (((0,), (0,)), ((), ()))
    w_in[...] = lax.dot_general(proj_in_t[...], place_in, columns, preferred_element_type=f32).astype(bf16)
    w_out[...] = lax.dot_general(proj_out_t[...], place_out, columns, preferred_element_type=f32).astype(bf16)

    half_columns = pl.ds(pl.multiple_of(core * 1024, 1024), 1024)
    swap_out = remote(
        query_grads.at[pl.ds(pl.multiple_of((1 - core) * 32, 32), 32)],
        queries.at[here, :, half_columns],
        swap_sem.at[0], swap_sem.at[1], sibling,
    )
    swap_own = pltpu.make_async_copy(
        query_grads.at[pl.ds(pl.multiple_of(core * 32, 32), 32)],
        queries.at[here, :, half_columns],
        swap_sem.at[2],
    )

    pl.semaphore_wait(barrier, len(peers))
    swap_out.start()
    swap_own.start()

    def at(way, along, across):
        step_x, step_y = (along, across) if way == 0 else (across, along)
        return (x + step_x) % SIDE, (y + step_y) % SIDE

    def query_copy(way, owner, columns, index, to):
        rows = queries.at[owner[0] * SIDE + owner[1], pl.ds(way * 16, 16), columns]
        return remote(
            rows, rows, query_ssem.at[way * 19 + index], query_rsem.at[way * 16 + owner[0] * SIDE + owner[1]],
            device(*to, z, core),
        )

    every = pl.ds(0, 2048)

    def query_wait(way, along, across):
        query_copy(way, at(way, along, across), every, 0, at(way, 1, 0)).wait_recv()

    def spread_first():
        swap_own.wait()
        swap_out.wait()
        for index, along in enumerate((1, 3, 2)):
            for way in range(2):
                query_copy(way, at(way, 0, 0), every, index, at(way, along, 0)).start()
        for way in range(2):
            spread_second(way, 0)

    def spread_second(way, along):
        query_copy(way, at(way, along, 0), every, 3 + along * 4, at(way, 0, 1)).start()
        query_copy(way, at(way, along, 0), every, 4 + along * 4, at(way, 0, 3)).start()

    def pass_first():
        for along in (1, 3, 2):
            for way in range(2):
                query_wait(way, along, 0)
                spread_second(way, along)

    def pass_second(along):
        for way in range(2):
            query_wait(way, along, 3)
            query_copy(way, at(way, along, 3), pl.ds(0, 1024), 5 + along * 4, at(way, 0, 1)).start()
            query_wait(way, along, 1)
            query_copy(way, at(way, along, 1), pl.ds(1024, 1024), 6 + along * 4, at(way, 0, 3)).start()

    def opposite_second():
        for along in range(4):
            for way in range(2):
                query_wait(way, along, 2)

    def pass_both():
        pass_second(1)
        pass_second(3)

    query_steps = (spread_first, pass_first, lambda: pass_second(0), pass_both, lambda: pass_second(2))

    token = lax.broadcasted_iota(jnp.int32, (128, 128), 0)

    def pair_copy(chunk):
        return remote(pair_send.at[chunk], pair_recv.at[chunk], pair_ssem.at[chunk], pair_rsem.at[chunk], sibling)

    def reduce_copy(chunk, owner_hi, source_hi):
        to = device(x, y, owner_hi * 2 + 1 - z_lo, core)
        return remote(
            reduce_send.at[chunk, owner_hi], reduce_recv.at[chunk, source_hi],
            reduce_ssem.at[chunk * 2 + owner_hi], reduce_rsem.at[chunk * 2 + source_hi], to,
        )

    def project(chunk):
        for load in loads(chunk):
            load.wait()

        @pl.when(chunk + AHEAD < CHUNKS)
        def _():
            for load in loads(chunk + AHEAD):
                load.start()

        total = dot(out_held[chunk], w_out[...])
        total += dot(act_held[chunk], w_in[...])
        kept = []
        for place in range(4):
            owner = ((core + place // 2) % 2) * 2 + place % 2
            length = lengths[chunk * 4 + owner]
            kept.append(jnp.where(token < length, total[place * 128 : place * 128 + 128], 0.0))
        own_part[chunk, 0:128] = kept[0]
        own_part[chunk, 128:256] = kept[1]
        pair_send[chunk, 0:128] = kept[2]
        pair_send[chunk, 128:256] = kept[3]
        pair_copy(chunk).start()
    def reduce(chunk):
        pair_copy(chunk).wait_recv()
        for owner_hi in range(2):
            rows = slice(owner_hi * 128, owner_hi * 128 + 128)
            total = own_part[chunk, rows] + pair_recv[chunk, rows]
            largest = jnp.max(jnp.abs(total), axis=0, keepdims=True)
            power = jnp.floor(jnp.log2(jnp.maximum(largest, 1e-30))) + 1.0
            scaled = jnp.round(total * jnp.exp2(15.0 - power))
            coded = jnp.clip(scaled, -32767.0, 32767.0).astype(jnp.int32).astype(jnp.int16)
            reduce_send[chunk, owner_hi, 0:128] = coded
            reduce_send[chunk, owner_hi, 128:144] = jnp.broadcast_to(power, (16, 128)).astype(jnp.int32).astype(jnp.int16)
            reduce_copy(chunk, owner_hi, z_hi).start()

    def outer(chunk):
        for source_hi in range(2):
            reduce_copy(chunk, 0, source_hi).wait_recv()
        total = jnp.zeros((128, 128), f32)
        for source_hi in range(2):
            power = reduce_recv[chunk, source_hi, 128:144].astype(jnp.int32)[0:1].astype(f32)
            total += reduce_recv[chunk, source_hi, 0:128].astype(jnp.int32).astype(f32) * jnp.exp2(power - 15.0)
        sides = total.astype(bf16)
        wide = sides.astype(f32)
        lanes = lax.broadcasted_iota(jnp.int32, (128, 128), 1)
        in_twice = jnp.where(lanes < 64, pltpu.roll(wide, 64, 1), wide).astype(bf16)
        both = lax.dot_general(sides, in_twice, columns, preferred_element_type=f32)
        grads = jnp.where(lanes[0:32] < 64, both[0:32], both[32:64])
        squares = jnp.square(grads.astype(bf16).astype(f32))
        square = jnp.sum(jnp.sum(squares, axis=0, keepdims=True), axis=1, keepdims=True)
        scaled = (grads * (64.0 * lax.rsqrt(square + eps))).astype(bf16)
        grads_send[0, chunk] = scaled[0:16]
        grads_send[1, chunk] = scaled[16:32]

    def grads_copy(batch, index, peer, source, to):
        block, owner = source
        first, last = BATCHES[batch]
        rows = pl.ds(first, last - first)
        return remote(
            grads_send.at[peer[0] // 2, rows], grads_recv.at[block, rows, owner],
            grads_ssem.at[batch * 7 + index], grads_rsem.at[batch * 8 + block * 4 + owner], to,
        )

    def grads_out(batch):
        for i in range(7):
            grads_copy(batch, i, ring[i], grads_place(z, core), ring_ids[i]).start()

    def step(s, carry):
        pl.when(s < CHUNKS)(lambda: project(s))
        pl.when(s == QUERY_STEPS[0])(spread_first)
        pl.when((s >= REDUCE_LAG) & (s < CHUNKS + REDUCE_LAG))(lambda: reduce(s - REDUCE_LAG))
        for k in range(1, 5):
            pl.when(s == QUERY_STEPS[k])(query_steps[k])
        pl.when(s >= LAG)(lambda: outer(s - LAG))
        for batch, (first, last) in enumerate(BATCHES):
            pl.when(s == LAG + last - 1)(functools.partial(grads_out, batch))
        return carry

    lax.fori_loop(0, CHUNKS + LAG, step, 0)

    spread[...] = jnp.zeros_like(spread)
    query_row = lax.broadcasted_iota(jnp.int32, (32, 128), 0)
    query_lane = lax.broadcasted_iota(jnp.int32, (32, 128), 1)
    for source in range(8):
        shift = ((source // 2) % 2) * 64 + (source % 2) * 32
        pattern = (query_lane == query_row + shift).astype(bf16)
        for column in range(4):
            spread[source * 128 + column * 32 : source * 128 + column * 32 + 32, column * 128 : column * 128 + 128] = pattern

    opposite_second()

    own_place = part_place(z, core)

    def square_rows(block, carry):
        wide = queries[block].astype(f32)
        squares = wide * wide
        total = squares[:, 0:128]
        for column in range(1, 16):
            total += squares[:, column * 128 : column * 128 + 128]
        square_part[pl.ds(pl.multiple_of(block * 32, 32), 32)] = total
        return carry

    lax.fori_loop(0, 16, square_rows, 0)
    sums = lax.dot_general(
        jnp.ones((8, 128), f32), square_part[...], (((1,), (1,)), ((), ())),
        precision=lax.Precision.HIGHEST, preferred_element_type=f32,
    )
    row = lax.broadcasted_iota(jnp.int32, (8, 128), 0)
    squares = jnp.zeros((8, 128), f32)
    for group in range(4):
        squares = jnp.where(row == group, sums[:, group * 128 : group * 128 + 128], squares)
    square_send[...] = squares

    def square_copy(index, place, to):
        return remote(square_send, square_recv.at[place], square_ssem.at[index], square_rsem.at[place], to)

    for i in range(7):
        square_copy(i, own_place, ring_ids[i]).start()
    square_recv[own_place] = squares

    own_grads = grads_place(z, core)
    for n in range(CHUNKS):
        grads_recv[own_grads[0], n, own_grads[1]] = grads_send[z_hi, n]
    for batch in range(len(BATCHES)):
        for i in range(7):
            grads_copy(batch, i, ring[i], grads_place(*ring[i]), ring_ids[i]).wait_recv()
    grads_wide[...] = grads_recv[...].reshape(1024, 128).astype(f32)
    for j in range(16):
        train[:, j * 128 : j * 128 + 128] = grads_wide[pl.ds(j, 64, stride=16), :].astype(bf16)

    products = lax.dot_general(
        train[...], queries[...].reshape(512, 2048), (((1,), (1,)), ((), ())), preferred_element_type=f32
    )
    part_send[...] = products.astype(bf16).reshape(2, 32, 512)

    def part_copy(index, peer, place, to):
        return remote(
            part_send.at[peer[0] % 2], part_recv.at[place], part_ssem.at[index], part_rsem.at[place], to
        )

    for i in range(7):
        part_copy(i, ring[i], own_place, ring_ids[i]).start()
    part_recv[own_place] = part_send[z_lo]

    for chunk in range(CHUNKS):
        pair_copy(chunk).wait_send()
        for owner_hi in range(2):
            reduce_copy(chunk, owner_hi, 0).wait_send()
    for batch in range(len(BATCHES)):
        for i in range(7):
            grads_copy(batch, i, ring[i], own_grads, ring_ids[i]).wait_send()
    for way in range(2):
        for i in range(19):
            half = i >= 3 and i % 4 in (1, 2)
            query_copy(way, (x, y), pl.ds(0, 1024) if half else every, i, at(way, 1, 0)).wait_send()
    for i in range(7):
        square_copy(i, own_place, ring_ids[i]).wait_send()

    for i in range(7):
        square_copy(i, part_place(*ring[i]), ring_ids[i]).wait_recv()
    left = jnp.concatenate([square_recv[place] for place in range(8)], axis=1)
    pieces = []
    for _ in range(3):
        piece = left.astype(bf16)
        pieces.append(piece)
        left = left - piece.astype(f32)
    spread_squares = sum(dot(piece, spread[...]) for piece in pieces)
    scales = lax.rsqrt(spread_squares + eps)

    for i in range(7):
        part_copy(i, ring[i], part_place(*ring[i]), ring_ids[i]).wait_recv()
    for place in range(8):
        for group in range(4):
            part_rows[group * 32 : group * 32 + 32, place * 128 : place * 128 + 128] = part_recv[
                place, :, group * 128 : group * 128 + 128
            ]
    result = dot(part_rows[...], spread[...])
    for group in range(4):
        scores[:, group * 512 : group * 512 + 512] = result[group * 32 : group * 32 + 32] * scales[group : group + 1]
    for i in range(7):
        part_copy(i, ring[i], own_place, ring_ids[i]).wait_send()


def on_device(activations, out_grads, lengths, proj_in, proj_out, query_grads):
    dma = pltpu.SemaphoreType.DMA
    vmem = pl.BlockSpec(memory_space=pltpu.VMEM)
    hbm = pl.BlockSpec(memory_space=pltpu.HBM)
    return pl.pallas_call(
        kernel,
        out_shape=pltpu.VMEM((32, 2048), f32),
        in_specs=[hbm] * 6,
        out_specs=vmem,
        scratch_shapes=[
            pltpu.SMEM((32,), jnp.int32),
            pltpu.VMEM((64, 1024), bf16),
            pltpu.VMEM((64, 512), bf16),
            pltpu.VMEM((64, 2048), bf16),
            pltpu.VMEM((8, 512, 2048), bf16),
            pltpu.VMEM((8, 512, 512), bf16),
            pltpu.VMEM((2048, 128), bf16),
            pltpu.VMEM((512, 128), bf16),
            pltpu.VMEM((8, 256, 128), f32),
            pltpu.VMEM((8, 256, 128), f32),
            pltpu.VMEM((8, 256, 128), f32),
            pltpu.VMEM((8, 2, 144, 128), jnp.int16),
            pltpu.VMEM((8, 2, 144, 128), jnp.int16),
            pltpu.VMEM((2, 8, 16, 128), bf16),
            pltpu.VMEM((2, 8, 4, 16, 128), bf16),
            pltpu.VMEM((1024, 128), f32),
            pltpu.VMEM((64, 2048), bf16),
            pltpu.VMEM((16, 32, 2048), bf16),
            pltpu.VMEM((512, 128), f32),
            pltpu.VMEM((8, 128), f32),
            pltpu.VMEM((8, 8, 128), f32),
            pltpu.VMEM((2, 32, 512), bf16),
            pltpu.VMEM((8, 32, 512), bf16),
            pltpu.VMEM((128, 1024), bf16),
            pltpu.VMEM((1024, 512), bf16),
            dma((4,)),
            dma((32,)),
            dma((8,)),
            dma((8,)),
            dma((16,)),
            dma((16,)),
            dma((7 * len(BATCHES),)),
            dma((8 * len(BATCHES),)),
            dma((3,)),
            dma((38,)),
            dma((32,)),
            dma((7,)),
            dma((8,)),
            dma((7,)),
            dma((8,)),
        ],
        compiler_params=pltpu.CompilerParams(
            collective_id=0, has_side_effects=True, vmem_limit_bytes=50 * 2**20
        ),
    )(
        *(
            pltpu.with_memory_space_constraint(array, pltpu.HBM)
            for array in (
                lengths,
                out_grads.reshape(8, 512, 2048),
                activations.reshape(8, 512, 512),
                proj_in.T,
                proj_out.T,
                query_grads,
            )
        )
    )


def solution(mesh):
    placed = (
        P("dp", None, "tensor"),
        P("dp", None, "tensor"),
        P("dp"),
        P("tensor", None),
        P("tensor", None),
        P("dp", "tensor"),
    )
    return jax.shard_map(
        on_device, mesh=mesh, in_specs=placed, out_specs=P("dp", None), check_vma=False
    )
```

```python
import functools

import jax
import jax.numpy as jnp
from jax import lax
from jax.experimental import pallas as pl
from jax.experimental.pallas import tpu as pltpu
from jax.sharding import PartitionSpec as P

eps = 1e-06
f32 = jnp.float32
bf16 = jnp.bfloat16
MESH = pl.DeviceIdType.MESH

SIDE = 4
CHUNKS = 8
AHEAD = 3
REDUCE_LAG = 2
QUERY_STEPS = (1,5,8,10,12)
BATCHES = ((0, 4), (4, 7), (7, 8))
LAG = 8
RING = ((2, 0), (2, 1), (1, 0), (1, 1), (3, 0), (3, 1), (0, 1))


def dot(left, right):
    return jnp.dot(left, right, preferred_element_type=f32)


def kernel(
    lengths_in, out_grads, activations, proj_in_in, proj_out_in, queries_in,
    scores,
    lengths, query_grads, proj_in_t, proj_out_t, held_rows, weights,
    own_part, pair_send, pair_recv, reduce_send, reduce_recv,
    grads_send, grads_recv, grads_wide, train,
    queries, square_part, square_send, square_recv,
    part_send, part_recv, part_rows, spread,
    small_sem, load_sem, pair_ssem, pair_rsem, reduce_ssem, reduce_rsem,
    grads_ssem, grads_rsem, swap_sem,
    query_ssem, query_rsem,
    square_ssem, square_rsem, part_ssem, part_rsem,
):
    dp = lax.axis_index("dp")
    tensor = lax.axis_index("tensor")
    x, y, z_lo = dp // 8, (dp // 2) % 4, dp % 2
    z_hi, core = tensor // 2, tensor % 2
    z = z_hi * 2 + z_lo
    here = x * SIDE + y

    def device(x, y, z, core):
        return (x * 8 + y * 2 + z % 2, (z // 2) * 2 + core)

    def ring_peer(step_z, step_core):
        return (z + step_z) % SIDE, (core + step_core) % 2

    def grads_place(z, core):
        return 1 - z % 2, core * 2 + z // 2

    def part_place(z, core):
        return (z // 2) * 4 + (z % 2) * 2 + core

    sibling = device(x, y, z, 1 - core)
    ring = [ring_peer(*steps) for steps in RING]
    ring_ids = [device(x, y, *peer) for peer in ring]
    around_ids = [device((x + step) % SIDE, y, z, core) for step in (1, 2, 3)]
    around_ids += [device(x, (y + step) % SIDE, z, core) for step in (1, 2, 3)]

    def remote(src, dst, send_sem, recv_sem, to):
        return pltpu.make_async_remote_copy(
            src_ref=src, dst_ref=dst, send_sem=send_sem, recv_sem=recv_sem,
            device_id=to, device_id_type=MESH,
        )

    barrier = pltpu.get_barrier_semaphore()
    peers = ring_ids + around_ids
    for peer in peers:
        pl.semaphore_signal(barrier, inc=1, device_id=peer, device_id_type=MESH)

    def loads(chunk):
        for half in range(2):
            rows = pl.ds(pl.multiple_of((core + half) % 2 * 256, 256), 256)
            held = pl.ds(half * 256, 256)
            yield pltpu.make_async_copy(
                out_grads.at[chunk, rows], held_rows.at[chunk, held, pl.ds(0, 2048)], load_sem.at[chunk * 4 + half]
            )
            yield pltpu.make_async_copy(
                activations.at[chunk, rows], held_rows.at[chunk, held, pl.ds(2048, 512)], load_sem.at[chunk * 4 + 2 + half]
            )

    small = [
        pltpu.make_async_copy(proj_out_in, proj_out_t, small_sem.at[0]),
        pltpu.make_async_copy(proj_in_in, proj_in_t, small_sem.at[1]),
        pltpu.make_async_copy(lengths_in, lengths, small_sem.at[2]),
        pltpu.make_async_copy(queries_in, query_grads, small_sem.at[3]),
    ]
    for load in small + list(loads(0)):
        load.start()
    for load in small[:2]:
        load.wait()
    for chunk in range(1, AHEAD):
        for load in loads(chunk):
            load.start()

    rank_row = lax.broadcasted_iota(jnp.int32, (64, 128), 0)
    lane = lax.broadcasted_iota(jnp.int32, (64, 128), 1)
    place_out = (lane == (rank_row % 2) * 32 + rank_row // 2).astype(bf16)
    place_in = (lane == rank_row + 64).astype(bf16)
    columns = (((0,), (0,)), ((), ()))
    weights[2048:2560] = lax.dot_general(proj_in_t[...], place_in, columns, preferred_element_type=f32).astype(bf16)
    weights[0:2048] = lax.dot_general(proj_out_t[...], place_out, columns, preferred_element_type=f32).astype(bf16)
    for load in small[2:]:
        load.wait()

    half_columns = pl.ds(pl.multiple_of(core * 1024, 1024), 1024)
    swap_out = remote(
        query_grads.at[pl.ds(pl.multiple_of((1 - core) * 32, 32), 32)],
        queries.at[here, :, half_columns],
        swap_sem.at[0], swap_sem.at[1], sibling,
    )
    swap_own = pltpu.make_async_copy(
        query_grads.at[pl.ds(pl.multiple_of(core * 32, 32), 32)],
        queries.at[here, :, half_columns],
        swap_sem.at[2],
    )

    def at(way, along, across):
        step_x, step_y = (along, across) if way == 0 else (across, along)
        return (x + step_x) % SIDE, (y + step_y) % SIDE

    def query_copy(way, owner, columns, index, to):
        rows = queries.at[owner[0] * SIDE + owner[1], pl.ds(way * 16, 16), columns]
        return remote(
            rows, rows, query_ssem.at[way * 19 + index], query_rsem.at[way * 16 + owner[0] * SIDE + owner[1]],
            device(*to, z, core),
        )

    every = pl.ds(0, 2048)

    def query_wait(way, along, across):
        query_copy(way, at(way, along, across), every, 0, at(way, 1, 0)).wait_recv()

    def spread_first():
        swap_own.wait()
        swap_out.wait()
        for index, along in enumerate((1, 3, 2)):
            for way in range(2):
                query_copy(way, at(way, 0, 0), every, index, at(way, along, 0)).start()
        for way in range(2):
            spread_second(way, 0)

    def spread_second(way, along):
        query_copy(way, at(way, along, 0), every, 3 + along * 4, at(way, 0, 1)).start()
        query_copy(way, at(way, along, 0), every, 4 + along * 4, at(way, 0, 3)).start()

    def pass_first():
        for along in (1, 3, 2):
            for way in range(2):
                query_wait(way, along, 0)
                spread_second(way, along)

    def pass_second(along):
        for way in range(2):
            query_wait(way, along, 3)
            query_copy(way, at(way, along, 3), pl.ds(0, 1024), 5 + along * 4, at(way, 0, 1)).start()
            query_wait(way, along, 1)
            query_copy(way, at(way, along, 1), pl.ds(1024, 1024), 6 + along * 4, at(way, 0, 3)).start()

    def opposite_second():
        for along in range(4):
            for way in range(2):
                query_wait(way, along, 2)

    def pass_both():
        pass_second(1)
        pass_second(3)

    query_steps = (spread_first, pass_first, lambda: pass_second(0), pass_both, lambda: pass_second(2))

    token = lax.broadcasted_iota(jnp.int32, (128, 128), 0)

    def pair_copy(chunk):
        return remote(pair_send.at[chunk], pair_recv.at[chunk], pair_ssem.at[chunk], pair_rsem.at[chunk], sibling)

    def reduce_copy(chunk, owner_hi, source_hi):
        to = device(x, y, owner_hi * 2 + 1 - z_lo, core)
        return remote(
            reduce_send.at[chunk, owner_hi], reduce_recv.at[chunk, source_hi],
            reduce_ssem.at[chunk * 2 + owner_hi], reduce_rsem.at[chunk * 2 + source_hi], to,
        )

    def project(chunk):
        for load in loads(chunk):
            load.wait()

        @pl.when(chunk + AHEAD < CHUNKS)
        def _():
            for load in loads(chunk + AHEAD):
                load.start()

        total = dot(held_rows[chunk], weights[...])
        kept = []
        for place in range(4):
            owner = ((core + place // 2) % 2) * 2 + place % 2
            length = lengths[chunk * 4 + owner]
            kept.append(jnp.where(token < length, total[place * 128 : place * 128 + 128], 0.0))
        own_part[chunk, 0:128] = kept[0]
        own_part[chunk, 128:256] = kept[1]
        pair_send[chunk, 0:128] = kept[2]
        pair_send[chunk, 128:256] = kept[3]

        @pl.when(chunk == 0)
        def _():
            pl.semaphore_wait(barrier, len(peers))
            swap_out.start()
            swap_own.start()

        pair_copy(chunk).start()
    def reduce(chunk):
        pair_copy(chunk).wait_recv()
        for owner_hi in range(2):
            rows = slice(owner_hi * 128, owner_hi * 128 + 128)
            total = own_part[chunk, rows] + pair_recv[chunk, rows]
            largest = jnp.max(jnp.abs(total), axis=0, keepdims=True)
            power = jnp.floor(jnp.log2(jnp.maximum(largest, 1e-30))) + 1.0
            scaled = jnp.round(total * jnp.exp2(15.0 - power))
            coded = jnp.clip(scaled, -32767.0, 32767.0).astype(jnp.int32).astype(jnp.int16)
            reduce_send[chunk, owner_hi, 0:128] = coded
            reduce_send[chunk, owner_hi, 128:144] = jnp.broadcast_to(power, (16, 128)).astype(jnp.int32).astype(jnp.int16)
            reduce_copy(chunk, owner_hi, z_hi).start()

    def outer(chunk):
        for source_hi in range(2):
            reduce_copy(chunk, 0, source_hi).wait_recv()
        total = jnp.zeros((128, 128), f32)
        for source_hi in range(2):
            power = reduce_recv[chunk, source_hi, 128:144].astype(jnp.int32)[0:1].astype(f32)
            total += reduce_recv[chunk, source_hi, 0:128].astype(jnp.int32).astype(f32) * jnp.exp2(power - 15.0)
        sides = total.astype(bf16)
        wide = sides.astype(f32)
        lanes = lax.broadcasted_iota(jnp.int32, (128, 128), 1)
        in_twice = jnp.where(lanes < 64, pltpu.roll(wide, 64, 1), wide).astype(bf16)
        both = lax.dot_general(sides, in_twice, columns, preferred_element_type=f32)
        grads = jnp.where(lanes[0:32] < 64, both[0:32], both[32:64])
        squares = jnp.square(grads.astype(bf16).astype(f32))
        square = jnp.sum(jnp.sum(squares, axis=0, keepdims=True), axis=1, keepdims=True)
        scaled = (grads * (64.0 * lax.rsqrt(square + eps))).astype(bf16)
        grads_send[0, chunk] = scaled[0:16]
        grads_send[1, chunk] = scaled[16:32]

    def grads_copy(batch, index, peer, source, to):
        block, owner = source
        first, last = BATCHES[batch]
        rows = pl.ds(first, last - first)
        return remote(
            grads_send.at[peer[0] // 2, rows], grads_recv.at[block, rows, owner],
            grads_ssem.at[batch * 7 + index], grads_rsem.at[batch * 8 + block * 4 + owner], to,
        )

    def grads_out(batch):
        for i in range(7):
            grads_copy(batch, i, ring[i], grads_place(z, core), ring_ids[i]).start()

    def step(s, carry):
        pl.when(s < CHUNKS)(lambda: project(s))
        pl.when(s == QUERY_STEPS[0])(spread_first)
        pl.when((s >= REDUCE_LAG) & (s < CHUNKS + REDUCE_LAG))(lambda: reduce(s - REDUCE_LAG))
        for k in range(1, 5):
            pl.when(s == QUERY_STEPS[k])(query_steps[k])
        pl.when(s >= LAG)(lambda: outer(s - LAG))
        for batch, (first, last) in enumerate(BATCHES):
            pl.when(s == LAG + last - 1)(functools.partial(grads_out, batch))
        return carry

    lax.fori_loop(0, CHUNKS + LAG, step, 0)

    spread[...] = jnp.zeros_like(spread)
    query_row = lax.broadcasted_iota(jnp.int32, (32, 128), 0)
    query_lane = lax.broadcasted_iota(jnp.int32, (32, 128), 1)
    for source in range(8):
        shift = ((source // 2) % 2) * 64 + (source % 2) * 32
        pattern = (query_lane == query_row + shift).astype(bf16)
        for column in range(4):
            spread[source * 128 + column * 32 : source * 128 + column * 32 + 32, column * 128 : column * 128 + 128] = pattern


    own_place = part_place(z, core)

    def square_rows(way, across):
        def one(along, carry):
            owner_x, owner_y = at(way, along, across)
            owner = owner_x * SIDE + owner_y
            wide = queries[owner, way * 16 : way * 16 + 16].astype(f32)
            squares = wide * wide
            total = squares[:, 0:128]
            for column in range(1, 16):
                total += squares[:, column * 128 : column * 128 + 128]
            square_part[pl.ds(pl.multiple_of(owner * 32 + way * 16, 16), 16)] = total
            return carry

        lax.fori_loop(0, SIDE, one, 0)

    for way in range(2):
        for across in (0, 1, 3):
            square_rows(way, across)
    opposite_second()
    for way in range(2):
        square_rows(way, 2)
    sums = lax.dot_general(
        jnp.ones((8, 128), f32), square_part[...], (((1,), (1,)), ((), ())),
        precision=lax.Precision.HIGHEST, preferred_element_type=f32,
    )
    row = lax.broadcasted_iota(jnp.int32, (8, 128), 0)
    squares = jnp.zeros((8, 128), f32)
    for group in range(4):
        squares = jnp.where(row == group, sums[:, group * 128 : group * 128 + 128], squares)
    square_send[...] = squares

    def square_copy(index, place, to):
        return remote(square_send, square_recv.at[place], square_ssem.at[index], square_rsem.at[place], to)

    for i in range(7):
        square_copy(i, own_place, ring_ids[i]).start()
    square_recv[own_place] = squares

    own_grads = grads_place(z, core)
    for n in range(CHUNKS):
        grads_recv[own_grads[0], n, own_grads[1]] = grads_send[z_hi, n]
    for batch in range(len(BATCHES)):
        for i in range(7):
            grads_copy(batch, i, ring[i], grads_place(*ring[i]), ring_ids[i]).wait_recv()
    grads_wide[...] = grads_recv[...].reshape(1024, 128).astype(f32)
    for j in range(16):
        train[:, j * 128 : j * 128 + 128] = grads_wide[pl.ds(j, 64, stride=16), :].astype(bf16)

    def part_copy(half, index, peer, place, to):
        return remote(
            part_send.at[half, peer[0] % 2], part_recv.at[half, place],
            part_ssem.at[half * 7 + index], part_rsem.at[half * 8 + place], to,
        )

    for half in range(2):
        products = lax.dot_general(
            train[...], queries[half * 8 : half * 8 + 8].reshape(256, 2048), (((1,), (1,)), ((), ())),
            preferred_element_type=f32,
        )
        part_send[half] = products.astype(bf16).reshape(2, 32, 256)
        for i in range(7):
            part_copy(half, i, ring[i], own_place, ring_ids[i]).start()
        part_recv[half, own_place] = part_send[half, z_lo]

    for chunk in range(CHUNKS):
        pair_copy(chunk).wait_send()
        for owner_hi in range(2):
            reduce_copy(chunk, owner_hi, 0).wait_send()
    for batch in range(len(BATCHES)):
        for i in range(7):
            grads_copy(batch, i, ring[i], own_grads, ring_ids[i]).wait_send()
    for way in range(2):
        for i in range(19):
            half = i >= 3 and i % 4 in (1, 2)
            query_copy(way, (x, y), pl.ds(0, 1024) if half else every, i, at(way, 1, 0)).wait_send()
    for i in range(7):
        square_copy(i, own_place, ring_ids[i]).wait_send()

    for i in range(7):
        square_copy(i, part_place(*ring[i]), ring_ids[i]).wait_recv()
    left = jnp.concatenate([square_recv[place] for place in range(8)], axis=1)
    pieces = []
    for _ in range(3):
        piece = left.astype(bf16)
        pieces.append(piece)
        left = left - piece.astype(f32)
    spread_squares = sum(dot(piece, spread[...]) for piece in pieces)
    scales = lax.rsqrt(spread_squares + eps)

    for half in range(2):
        for i in range(7):
            part_copy(half, i, ring[i], part_place(*ring[i]), ring_ids[i]).wait_recv()
        for place in range(8):
            for group in range(2):
                part_rows[half, group * 32 : group * 32 + 32, place * 128 : place * 128 + 128] = part_recv[
                    half, place, :, group * 128 : group * 128 + 128
                ]
        result = dot(part_rows[half], spread[...])
        for group in range(2):
            first = half * 2 + group
            scores[:, first * 512 : first * 512 + 512] = (
                result[group * 32 : group * 32 + 32] * scales[first : first + 1]
            )

    for i in range(7):
        for half in range(2):
            part_copy(half, i, ring[i], own_place, ring_ids[i]).wait_send()


def on_device(activations, out_grads, lengths, proj_in, proj_out, query_grads):
    dma = pltpu.SemaphoreType.DMA
    vmem = pl.BlockSpec(memory_space=pltpu.VMEM)
    hbm = pl.BlockSpec(memory_space=pltpu.HBM)
    return pl.pallas_call(
        kernel,
        out_shape=pltpu.VMEM((32, 2048), f32),
        in_specs=[hbm] * 6,
        out_specs=vmem,
        scratch_shapes=[
            pltpu.SMEM((32,), jnp.int32),
            pltpu.VMEM((64, 1024), bf16),
            pltpu.VMEM((64, 512), bf16),
            pltpu.VMEM((64, 2048), bf16),
            pltpu.VMEM((8, 512, 2560), bf16),
            pltpu.VMEM((2560, 128), bf16),
            pltpu.VMEM((8, 256, 128), f32),
            pltpu.VMEM((8, 256, 128), f32),
            pltpu.VMEM((8, 256, 128), f32),
            pltpu.VMEM((8, 2, 144, 128), jnp.int16),
            pltpu.VMEM((8, 2, 144, 128), jnp.int16),
            pltpu.VMEM((2, 8, 16, 128), bf16),
            pltpu.VMEM((2, 8, 4, 16, 128), bf16),
            pltpu.VMEM((1024, 128), f32),
            pltpu.VMEM((64, 2048), bf16),
            pltpu.VMEM((16, 32, 2048), bf16),
            pltpu.VMEM((512, 128), f32),
            pltpu.VMEM((8, 128), f32),
            pltpu.VMEM((8, 8, 128), f32),
            pltpu.VMEM((2, 2, 32, 256), bf16),
            pltpu.VMEM((2, 8, 32, 256), bf16),
            pltpu.VMEM((2, 64, 1024), bf16),
            pltpu.VMEM((1024, 512), bf16),
            dma((4,)),
            dma((32,)),
            dma((8,)),
            dma((8,)),
            dma((16,)),
            dma((16,)),
            dma((7 * len(BATCHES),)),
            dma((8 * len(BATCHES),)),
            dma((3,)),
            dma((38,)),
            dma((32,)),
            dma((7,)),
            dma((8,)),
            dma((14,)),
            dma((16,)),
        ],
        compiler_params=pltpu.CompilerParams(
            collective_id=0, has_side_effects=True, vmem_limit_bytes=50 * 2**20
        ),
    )(
        *(
            pltpu.with_memory_space_constraint(array, pltpu.HBM)
            for array in (
                lengths,
                out_grads.reshape(8, 512, 2048),
                activations.reshape(8, 512, 512),
                proj_in.T,
                proj_out.T,
                query_grads,
            )
        )
    )


def solution(mesh):
    placed = (
        P("dp", None, "tensor"),
        P("dp", None, "tensor"),
        P("dp"),
        P("tensor", None),
        P("tensor", None),
        P("dp", "tensor"),
    )
    return jax.shard_map(
        on_device, mesh=mesh, in_specs=placed, out_specs=P("dp", None), check_vma=False
    )
```

```python
import functools

import jax
import jax.numpy as jnp
from jax import lax
from jax.experimental import pallas as pl
from jax.experimental.pallas import tpu as pltpu
from jax.sharding import PartitionSpec as P

eps = 1e-06
f32 = jnp.float32
bf16 = jnp.bfloat16
MESH = pl.DeviceIdType.MESH

SIDE = 4
CHUNKS = 8
AHEAD = 3
REDUCE_LAG = 2
QUERY_STEPS = (1,5,8,10,12)
BATCHES = ((0, 4), (4, 7), (7, 8))
LAG = 8
RING = ((2, 0), (2, 1), (1, 0), (1, 1), (3, 0), (3, 1), (0, 1))


def dot(left, right):
    return jnp.dot(left, right, preferred_element_type=f32)


def kernel(
    lengths_in, out_grads, activations, proj_in_in, proj_out_in, queries_in,
    scores,
    lengths, query_grads, proj_in_t, proj_out_t, held_rows, weights,
    own_part, pair_send, pair_recv, reduce_send, reduce_recv,
    grads_send, grads_recv, grads_wide, train,
    queries, square_part, square_send, square_recv,
    part_send, part_recv, part_rows, spread,
    small_sem, load_sem, pair_ssem, pair_rsem, reduce_ssem, reduce_rsem,
    grads_ssem, grads_rsem, swap_sem,
    query_ssem, query_rsem,
    square_ssem, square_rsem, part_ssem, part_rsem,
):
    dp = lax.axis_index("dp")
    tensor = lax.axis_index("tensor")
    x, y, z_lo = dp // 8, (dp // 2) % 4, dp % 2
    z_hi, core = tensor // 2, tensor % 2
    z = z_hi * 2 + z_lo
    here = x * SIDE + y

    def device(x, y, z, core):
        return (x * 8 + y * 2 + z % 2, (z // 2) * 2 + core)

    def ring_peer(step_z, step_core):
        return (z + step_z) % SIDE, (core + step_core) % 2

    def grads_place(z, core):
        return 1 - z % 2, core * 2 + z // 2

    def part_place(z, core):
        return (z // 2) * 4 + (z % 2) * 2 + core

    sibling = device(x, y, z, 1 - core)
    ring = [ring_peer(*steps) for steps in RING]
    ring_ids = [device(x, y, *peer) for peer in ring]
    around_ids = [device((x + step) % SIDE, y, z, core) for step in (1, 2, 3)]
    around_ids += [device(x, (y + step) % SIDE, z, core) for step in (1, 2, 3)]

    def remote(src, dst, send_sem, recv_sem, to):
        return pltpu.make_async_remote_copy(
            src_ref=src, dst_ref=dst, send_sem=send_sem, recv_sem=recv_sem,
            device_id=to, device_id_type=MESH,
        )

    barrier = pltpu.get_barrier_semaphore()
    peers = ring_ids + around_ids
    for peer in peers:
        pl.semaphore_signal(barrier, inc=1, device_id=peer, device_id_type=MESH)

    def loads(chunk):
        for half in range(2):
            rows = pl.ds(pl.multiple_of((core + half) % 2 * 256, 256), 256)
            held = pl.ds(half * 256, 256)
            yield pltpu.make_async_copy(
                out_grads.at[chunk, rows], held_rows.at[chunk, held, pl.ds(0, 2048)], load_sem.at[chunk * 4 + half]
            )
            yield pltpu.make_async_copy(
                activations.at[chunk, rows], held_rows.at[chunk, held, pl.ds(2048, 512)], load_sem.at[chunk * 4 + 2 + half]
            )

    small = [
        pltpu.make_async_copy(proj_out_in, proj_out_t, small_sem.at[0]),
        pltpu.make_async_copy(proj_in_in, proj_in_t, small_sem.at[1]),
        pltpu.make_async_copy(lengths_in, lengths, small_sem.at[2]),
        pltpu.make_async_copy(queries_in, query_grads, small_sem.at[3]),
    ]
    for load in small + list(loads(0)):
        load.start()
    for load in small[:2]:
        load.wait()
    for chunk in range(1, AHEAD):
        for load in loads(chunk):
            load.start()

    rank_row = lax.broadcasted_iota(jnp.int32, (64, 128), 0)
    lane = lax.broadcasted_iota(jnp.int32, (64, 128), 1)
    place_out = (lane == (rank_row % 2) * 32 + rank_row // 2).astype(bf16)
    place_in = (lane == rank_row + 64).astype(bf16)
    columns = (((0,), (0,)), ((), ()))
    weights[2048:2560] = lax.dot_general(proj_in_t[...], place_in, columns, preferred_element_type=f32).astype(bf16)
    weights[0:2048] = lax.dot_general(proj_out_t[...], place_out, columns, preferred_element_type=f32).astype(bf16)
    for load in small[2:]:
        load.wait()

    half_columns = pl.ds(pl.multiple_of(core * 1024, 1024), 1024)
    swap_out = remote(
        query_grads.at[pl.ds(pl.multiple_of((1 - core) * 32, 32), 32)],
        queries.at[here, :, half_columns],
        swap_sem.at[0], swap_sem.at[1], sibling,
    )
    swap_own = pltpu.make_async_copy(
        query_grads.at[pl.ds(pl.multiple_of(core * 32, 32), 32)],
        queries.at[here, :, half_columns],
        swap_sem.at[2],
    )

    def at(way, along, across):
        step_x, step_y = (along, across) if way == 0 else (across, along)
        return (x + step_x) % SIDE, (y + step_y) % SIDE

    def query_copy(way, owner, columns, index, to):
        rows = queries.at[owner[0] * SIDE + owner[1], pl.ds(way * 16, 16), columns]
        return remote(
            rows, rows, query_ssem.at[way * 19 + index], query_rsem.at[way * 16 + owner[0] * SIDE + owner[1]],
            device(*to, z, core),
        )

    every = pl.ds(0, 2048)

    def query_wait(way, along, across):
        query_copy(way, at(way, along, across), every, 0, at(way, 1, 0)).wait_recv()

    def spread_first():
        swap_own.wait()
        swap_out.wait()
        for index, along in enumerate((1, 3, 2)):
            for way in range(2):
                query_copy(way, at(way, 0, 0), every, index, at(way, along, 0)).start()
        for way in range(2):
            spread_second(way, 0)

    def spread_second(way, along):
        query_copy(way, at(way, along, 0), every, 3 + along * 4, at(way, 0, 1)).start()
        query_copy(way, at(way, along, 0), every, 4 + along * 4, at(way, 0, 3)).start()

    def pass_first():
        for along in (1, 3, 2):
            for way in range(2):
                query_wait(way, along, 0)
                spread_second(way, along)

    def pass_second(along):
        for way in range(2):
            query_wait(way, along, 3)
            query_copy(way, at(way, along, 3), pl.ds(0, 1024), 5 + along * 4, at(way, 0, 1)).start()
            query_wait(way, along, 1)
            query_copy(way, at(way, along, 1), pl.ds(1024, 1024), 6 + along * 4, at(way, 0, 3)).start()

    def opposite_second():
        for along in range(4):
            for way in range(2):
                query_wait(way, along, 2)

    def pass_both():
        pass_second(1)
        pass_second(3)

    query_steps = (spread_first, pass_first, lambda: pass_second(0), pass_both, lambda: pass_second(2))

    token = lax.broadcasted_iota(jnp.int32, (128, 128), 0)

    def pair_copy(chunk):
        return remote(pair_send.at[chunk], pair_recv.at[chunk], pair_ssem.at[chunk], pair_rsem.at[chunk], sibling)

    def reduce_copy(chunk, owner_hi, source_hi):
        to = device(x, y, owner_hi * 2 + 1 - z_lo, core)
        return remote(
            reduce_send.at[chunk, owner_hi], reduce_recv.at[chunk, source_hi],
            reduce_ssem.at[chunk * 2 + owner_hi], reduce_rsem.at[chunk * 2 + source_hi], to,
        )

    def project(chunk):
        for load in loads(chunk):
            load.wait()

        @pl.when(chunk + AHEAD < CHUNKS)
        def _():
            for load in loads(chunk + AHEAD):
                load.start()

        total = dot(held_rows[chunk], weights[...])
        kept = []
        for place in range(4):
            owner = ((core + place // 2) % 2) * 2 + place % 2
            length = lengths[chunk * 4 + owner]
            kept.append(jnp.where(token < length, total[place * 128 : place * 128 + 128], 0.0))
        own_part[chunk, 0:128] = kept[0]
        own_part[chunk, 128:256] = kept[1]
        pair_send[chunk, 0:128] = kept[2]
        pair_send[chunk, 128:256] = kept[3]

        @pl.when(chunk == 0)
        def _():
            pl.semaphore_wait(barrier, len(peers))
            swap_out.start()
            swap_own.start()

        pair_copy(chunk).start()
    def reduce(chunk):
        pair_copy(chunk).wait_recv()
        for owner_hi in range(2):
            rows = slice(owner_hi * 128, owner_hi * 128 + 128)
            total = own_part[chunk, rows] + pair_recv[chunk, rows]
            largest = jnp.max(jnp.abs(total), axis=0, keepdims=True)
            power = jnp.floor(jnp.log2(jnp.maximum(largest, 1e-30))) + 1.0
            scaled = jnp.round(total * jnp.exp2(15.0 - power))
            coded = jnp.clip(scaled, -32767.0, 32767.0).astype(jnp.int32).astype(jnp.int16)
            reduce_send[chunk, owner_hi, 0:128] = coded
            reduce_send[chunk, owner_hi, 128:144] = jnp.broadcast_to(power, (16, 128)).astype(jnp.int32).astype(jnp.int16)
            reduce_copy(chunk, owner_hi, z_hi).start()

    def outer(chunk):
        for source_hi in range(2):
            reduce_copy(chunk, 0, source_hi).wait_recv()
        total = jnp.zeros((128, 128), f32)
        for source_hi in range(2):
            power = reduce_recv[chunk, source_hi, 128:144].astype(jnp.int32)[0:1].astype(f32)
            total += reduce_recv[chunk, source_hi, 0:128].astype(jnp.int32).astype(f32) * jnp.exp2(power - 15.0)
        sides = total.astype(bf16)
        wide = sides.astype(f32)
        lanes = lax.broadcasted_iota(jnp.int32, (128, 128), 1)
        in_twice = jnp.where(lanes < 64, pltpu.roll(wide, 64, 1), wide).astype(bf16)
        both = lax.dot_general(sides, in_twice, columns, preferred_element_type=f32)
        grads = jnp.where(lanes[0:32] < 64, both[0:32], both[32:64])
        squares = jnp.square(grads.astype(bf16).astype(f32))
        square = jnp.sum(jnp.sum(squares, axis=0, keepdims=True), axis=1, keepdims=True)
        scaled = (grads * (64.0 * lax.rsqrt(square + eps))).astype(bf16)
        grads_send[0, chunk] = scaled[0:16]
        grads_send[1, chunk] = scaled[16:32]

    def grads_copy(batch, index, peer, source, to):
        block, owner = source
        first, last = BATCHES[batch]
        rows = pl.ds(first, last - first)
        return remote(
            grads_send.at[peer[0] // 2, rows], grads_recv.at[block, rows, owner],
            grads_ssem.at[batch * 7 + index], grads_rsem.at[batch * 8 + block * 4 + owner], to,
        )

    def grads_out(batch):
        for i in range(7):
            grads_copy(batch, i, ring[i], grads_place(z, core), ring_ids[i]).start()

    def step(s, carry):
        pl.when(s < CHUNKS)(lambda: project(s))
        pl.when(s == QUERY_STEPS[0])(spread_first)
        pl.when((s >= REDUCE_LAG) & (s < CHUNKS + REDUCE_LAG))(lambda: reduce(s - REDUCE_LAG))
        for k in range(1, 5):
            pl.when(s == QUERY_STEPS[k])(query_steps[k])
        pl.when(s >= LAG)(lambda: outer(s - LAG))
        for batch, (first, last) in enumerate(BATCHES):
            pl.when(s == LAG + last - 1)(functools.partial(grads_out, batch))
        return carry

    lax.fori_loop(0, CHUNKS + LAG, step, 0)

    spread[...] = jnp.zeros_like(spread)
    query_row = lax.broadcasted_iota(jnp.int32, (32, 128), 0)
    query_lane = lax.broadcasted_iota(jnp.int32, (32, 128), 1)
    for source in range(8):
        shift = ((source // 2) % 2) * 64 + (source % 2) * 32
        pattern = (query_lane == query_row + shift).astype(bf16)
        for column in range(4):
            spread[source * 128 + column * 32 : source * 128 + column * 32 + 32, column * 128 : column * 128 + 128] = pattern


    own_place = part_place(z, core)

    def square_rows(way, across):
        def one(along, carry):
            owner_x, owner_y = at(way, along, across)
            owner = owner_x * SIDE + owner_y
            wide = queries[owner, way * 16 : way * 16 + 16].astype(f32)
            squares = wide * wide
            total = squares[:, 0:128]
            for column in range(1, 16):
                total += squares[:, column * 128 : column * 128 + 128]
            square_part[pl.ds(pl.multiple_of(owner * 32 + way * 16, 16), 16)] = total
            return carry

        lax.fori_loop(0, SIDE, one, 0)

    for way in range(2):
        for across in (0, 1, 3):
            square_rows(way, across)
    opposite_second()
    for way in range(2):
        square_rows(way, 2)
    sums = lax.dot_general(
        jnp.ones((8, 128), f32), square_part[...], (((1,), (1,)), ((), ())),
        precision=lax.Precision.HIGHEST, preferred_element_type=f32,
    )
    row = lax.broadcasted_iota(jnp.int32, (8, 128), 0)
    squares = jnp.zeros((8, 128), f32)
    for group in range(4):
        squares = jnp.where(row == group, sums[:, group * 128 : group * 128 + 128], squares)
    square_send[...] = squares

    def square_copy(index, place, to):
        return remote(square_send, square_recv.at[place], square_ssem.at[index], square_rsem.at[place], to)

    for i in range(7):
        square_copy(i, own_place, ring_ids[i]).start()
    square_recv[own_place] = squares

    own_grads = grads_place(z, core)
    for n in range(CHUNKS):
        grads_recv[own_grads[0], n, own_grads[1]] = grads_send[z_hi, n]
    for batch in range(len(BATCHES)):
        for i in range(7):
            grads_copy(batch, i, ring[i], grads_place(*ring[i]), ring_ids[i]).wait_recv()
        first, last = BATCHES[batch]
        for block in range(2):
            rows = slice(block * 512 + first * 64, block * 512 + last * 64)
            grads_wide[rows] = grads_recv[block, first:last].reshape((last - first) * 64, 128).astype(f32)
    for j in range(16):
        train[:, j * 128 : j * 128 + 128] = grads_wide[pl.ds(j, 64, stride=16), :].astype(bf16)

    def part_copy(half, index, peer, place, to):
        return remote(
            part_send.at[half, peer[0] % 2], part_recv.at[half, place],
            part_ssem.at[half * 7 + index], part_rsem.at[half * 8 + place], to,
        )

    for half in range(2):
        products = lax.dot_general(
            train[...], queries[half * 8 : half * 8 + 8].reshape(256, 2048), (((1,), (1,)), ((), ())),
            preferred_element_type=f32,
        )
        part_send[half] = products.astype(bf16).reshape(2, 32, 256)
        for i in range(7):
            part_copy(half, i, ring[i], own_place, ring_ids[i]).start()
        part_recv[half, own_place] = part_send[half, z_lo]

    for chunk in range(CHUNKS):
        pair_copy(chunk).wait_send()
        for owner_hi in range(2):
            reduce_copy(chunk, owner_hi, 0).wait_send()
    for batch in range(len(BATCHES)):
        for i in range(7):
            grads_copy(batch, i, ring[i], own_grads, ring_ids[i]).wait_send()
    for way in range(2):
        for i in range(19):
            half = i >= 3 and i % 4 in (1, 2)
            query_copy(way, (x, y), pl.ds(0, 1024) if half else every, i, at(way, 1, 0)).wait_send()
    for i in range(7):
        square_copy(i, own_place, ring_ids[i]).wait_send()

    for i in range(7):
        square_copy(i, part_place(*ring[i]), ring_ids[i]).wait_recv()
    left = jnp.concatenate([square_recv[place] for place in range(8)], axis=1)
    pieces = []
    for _ in range(3):
        piece = left.astype(bf16)
        pieces.append(piece)
        left = left - piece.astype(f32)
    spread_squares = sum(dot(piece, spread[...]) for piece in pieces)
    scales = lax.rsqrt(spread_squares + eps)

    for half in range(2):
        for i in range(7):
            part_copy(half, i, ring[i], part_place(*ring[i]), ring_ids[i]).wait_recv()
        for place in range(8):
            for group in range(2):
                part_rows[half, group * 32 : group * 32 + 32, place * 128 : place * 128 + 128] = part_recv[
                    half, place, :, group * 128 : group * 128 + 128
                ]
        result = dot(part_rows[half], spread[...])
        for group in range(2):
            first = half * 2 + group
            scores[:, first * 512 : first * 512 + 512] = (
                result[group * 32 : group * 32 + 32] * scales[first : first + 1]
            )

    for i in range(7):
        for half in range(2):
            part_copy(half, i, ring[i], own_place, ring_ids[i]).wait_send()


def on_device(activations, out_grads, lengths, proj_in, proj_out, query_grads):
    dma = pltpu.SemaphoreType.DMA
    vmem = pl.BlockSpec(memory_space=pltpu.VMEM)
    hbm = pl.BlockSpec(memory_space=pltpu.HBM)
    return pl.pallas_call(
        kernel,
        out_shape=pltpu.VMEM((32, 2048), f32),
        in_specs=[hbm] * 6,
        out_specs=vmem,
        scratch_shapes=[
            pltpu.SMEM((32,), jnp.int32),
            pltpu.VMEM((64, 1024), bf16),
            pltpu.VMEM((64, 512), bf16),
            pltpu.VMEM((64, 2048), bf16),
            pltpu.VMEM((8, 512, 2560), bf16),
            pltpu.VMEM((2560, 128), bf16),
            pltpu.VMEM((8, 256, 128), f32),
            pltpu.VMEM((8, 256, 128), f32),
            pltpu.VMEM((8, 256, 128), f32),
            pltpu.VMEM((8, 2, 144, 128), jnp.int16),
            pltpu.VMEM((8, 2, 144, 128), jnp.int16),
            pltpu.VMEM((2, 8, 16, 128), bf16),
            pltpu.VMEM((2, 8, 4, 16, 128), bf16),
            pltpu.VMEM((1024, 128), f32),
            pltpu.VMEM((64, 2048), bf16),
            pltpu.VMEM((16, 32, 2048), bf16),
            pltpu.VMEM((512, 128), f32),
            pltpu.VMEM((8, 128), f32),
            pltpu.VMEM((8, 8, 128), f32),
            pltpu.VMEM((2, 2, 32, 256), bf16),
            pltpu.VMEM((2, 8, 32, 256), bf16),
            pltpu.VMEM((2, 64, 1024), bf16),
            pltpu.VMEM((1024, 512), bf16),
            dma((4,)),
            dma((32,)),
            dma((8,)),
            dma((8,)),
            dma((16,)),
            dma((16,)),
            dma((7 * len(BATCHES),)),
            dma((8 * len(BATCHES),)),
            dma((3,)),
            dma((38,)),
            dma((32,)),
            dma((7,)),
            dma((8,)),
            dma((14,)),
            dma((16,)),
        ],
        compiler_params=pltpu.CompilerParams(
            collective_id=0, has_side_effects=True, vmem_limit_bytes=50 * 2**20
        ),
    )(
        *(
            pltpu.with_memory_space_constraint(array, pltpu.HBM)
            for array in (
                lengths,
                out_grads.reshape(8, 512, 2048),
                activations.reshape(8, 512, 512),
                proj_in.T,
                proj_out.T,
                query_grads,
            )
        )
    )


def solution(mesh):
    placed = (
        P("dp", None, "tensor"),
        P("dp", None, "tensor"),
        P("dp"),
        P("tensor", None),
        P("tensor", None),
        P("dp", "tensor"),
    )
    return jax.shard_map(
        on_device, mesh=mesh, in_specs=placed, out_specs=P("dp", None), check_vma=False
    )
```
